32 devices in a mesh: gx: 4 (over y, core), gy: 8 (over z, x).
Axes of the slice: x: 2, y: 2, z: 4, core: 2. Of those that a mesh axis runs over, the one named last changes fastest.
Arguments:
- flow_pops: float32 [19, 2, 256, 1024], P(None, None, 'gx', 'gy'), may hold values from 0 to 0.8, as said below
- thermal_distributions: float32 [7, 2, 256, 1024], P(None, None, 'gx', 'gy'), may hold values from 0 to 0.6, as said below
- solid_mask: int32 [2, 256, 1024], P(None, 'gx', 'gy'), may hold values from 0 to 2, as said below
- link_flags: int32 [18, 2, 256, 1024], P(None, None, 'gx', 'gy'), may hold values from 0 to 1, as said below
Outputs:
- flow_final: float32 [19, 2, 256, 1024], P(None, None, 'gx', 'gy')
- heat_final: float32 [7, 2, 256, 1024], P(None, None, 'gx', 'gy')
The draws below stay inside these ranges and needn't reach their ends.
Inputs may be any that keep to these rules, and one draw needn't show every extreme that they name: `flow_pops`: populations positive, of the order of w_q. `thermal_distributions`: positive, about v_i times a temperature; solid cells hotter than fluid ones. `solid_mask`: solid cells form discs in each z layer (sections of the bed's spheres). `link_flags`: consistent with solid_mask: entry q-1 at cell r is 1 exactly where r - c_q is solid or outside the bed in x or y, z periodic.
All inputs are finite; a program needn't handle non-finite values.
Results may differ from the reference program's by a relative error of at most 0.0001.
Values sent between devices are 32-bit elements; how exact they have to be, the bound alone decides.
A program may use at most 128 MiB of HBM per device.

```python
import jax
import jax.numpy as jnp
import numpy as np

NODES_WRAPPED = 2
STEPS = 12
NODES_LENGTHWISE = 256
NODES_CROSSWISE = 1024


flow_velocity = np.array([[0, 0, 0], [1, 0, 0], [-1, 0, 0], [0, 1, 0], [0, -1, 0], [0, 0, 1], [0, 0, -1], [1, 1, 0], [-1, -1, 0], [1, -1, 0], [-1, 1, 0], [1, 0, 1], [-1, 0, -1], [1, 0, -1], [-1, 0, 1], [0, 1, 1], [0, -1, -1], [0, 1, -1], [0, -1, 1]])


flow_weight = np.array([1.0 / 3.0] + [1.0 / 18.0] * 6 + [1.0 / 36.0] * 12)


thermal_quadrature_share = np.array([0.25] + [0.125] * 6)


spacing = 16


def bed_layout(key):
    blocks_x = (NODES_LENGTHWISE + spacing - 1) // spacing
    blocks_y = (NODES_CROSSWISE + spacing - 1) // spacing
    keys = jax.random.split(key, 5)
    offset_x = jax.random.randint(keys[0], (blocks_x, blocks_y), -2, 3)
    offset_y = jax.random.randint(keys[1], (blocks_x, blocks_y), -2, 3)
    radius_sq = jax.random.randint(keys[2], (blocks_x, blocks_y), 4, 50)
    tilted = jax.random.randint(keys[3], (blocks_x, blocks_y), 0, 11)
    phases = jax.random.randint(keys[4], (blocks_x, blocks_y), 1, 3)
    x_cells = jnp.arange(NODES_LENGTHWISE, dtype=jnp.int32).reshape(1, NODES_LENGTHWISE, 1)
    y_cells = jnp.arange(NODES_CROSSWISE, dtype=jnp.int32).reshape(1, 1, NODES_CROSSWISE)
    z_cells = jnp.arange(NODES_WRAPPED, dtype=jnp.int32).reshape(NODES_WRAPPED, 1, 1)
    block_x = x_cells // spacing
    block_y = y_cells // spacing
    centre_x = block_x * spacing + spacing // 2 + offset_x[block_x, block_y]
    centre_y = block_y * spacing + spacing // 2 + offset_y[block_x, block_y]
    distance = (x_cells - centre_x) ** 2 + (y_cells - centre_y) ** 2 + z_cells * tilted[block_x, block_y]
    solid = distance < radius_sq[block_x, block_y]
    solid_node_flag = jnp.where(solid, phases[block_x, block_y], 0).astype(jnp.int32)
    blocked = jnp.pad(solid_node_flag != 0, ((0, 0), (1, 1), (1, 1)), constant_values=True)
    flags = []
    for link in range(1, 19):
        step_x, step_y, step_z = [int(entry) for entry in flow_velocity[link]]
        segment = blocked[:, 1 - step_x:1 - step_x + NODES_LENGTHWISE, 1 - step_y:1 - step_y + NODES_CROSSWISE]
        flags.append(jnp.roll(segment, step_z, axis=0))
    return (solid_node_flag, jnp.stack(flags).astype(jnp.int32))


def draw_solid_mask(key, part):
    solid_node_flag, flags = bed_layout(key)
    return solid_node_flag


def draw_link_flags(key, part):
    solid_node_flag, flags = bed_layout(key)
    return flags


def draw_flow_pops(key, part):
    key = jax.random.fold_in(key, 7)
    keys = jax.random.split(key, 5)
    cells = (NODES_WRAPPED, NODES_LENGTHWISE, NODES_CROSSWISE)
    shape = (19, NODES_WRAPPED, NODES_LENGTHWISE, NODES_CROSSWISE)
    x_share = (jnp.arange(NODES_LENGTHWISE, dtype=jnp.float32) + 0.5).reshape(1, NODES_LENGTHWISE, 1) / NODES_LENGTHWISE
    density = (1.2 - 0.4 * x_share) * jax.random.uniform(keys[0], cells, jnp.float32, 0.9, 1.1)
    speed_x = 0.1 * jax.random.uniform(keys[1], cells, jnp.float32, 0.6, 1.4)
    multiplier_value = jax.random.uniform(keys[4], shape, jnp.float32, 0.8, 1.2)
    speed_y = jax.random.uniform(keys[2], cells, jnp.float32, -0.04, 0.04)
    speed_z = jax.random.uniform(keys[3], cells, jnp.float32, -0.03, 0.03)
    quadrature_shares = jnp.asarray(flow_weight, jnp.float32).reshape(19, 1, 1, 1)
    along_x = jnp.asarray(flow_velocity[:, 0], jnp.float32).reshape(19, 1, 1, 1)
    along_y = jnp.asarray(flow_velocity[:, 1], jnp.float32).reshape(19, 1, 1, 1)
    along_z = jnp.asarray(flow_velocity[:, 2], jnp.float32).reshape(19, 1, 1, 1)
    projected = along_x * speed_x + along_y * speed_y + along_z * speed_z
    squared = speed_x * speed_x + speed_y * speed_y + speed_z * speed_z
    balance = quadrature_shares * density * (1.0 + 3.0 * projected + 4.5 * projected * projected - 1.5 * squared)
    return (balance * multiplier_value).astype(jnp.float32)


def draw_thermal_distributions(key, part):
    solid_node_flag, flags = bed_layout(key)
    key = jax.random.fold_in(key, 11)
    leading_element, second = jax.random.split(key)
    node_warmth = jnp.where(solid_node_flag == 0, 0.1, 1.0) * jax.random.uniform(leading_element, (NODES_WRAPPED, NODES_LENGTHWISE, NODES_CROSSWISE), jnp.float32, 0.8, 1.2)
    multiplier_value = jax.random.uniform(second, (7, NODES_WRAPPED, NODES_LENGTHWISE, NODES_CROSSWISE), jnp.float32, 0.8, 1.2)
    quadrature_shares = jnp.asarray(thermal_quadrature_share, jnp.float32).reshape(7, 1, 1, 1)
    return (quadrature_shares * node_warmth * multiplier_value).astype(jnp.float32)


def setup_inputs(seed: int = 0) -> dict:
    key_of = jax.random.split(jax.random.key(seed), 5)
    return {
        "flow_pops": draw_flow_pops(jax.random.fold_in(key_of[4], 71), 0),
        "thermal_distributions": draw_thermal_distributions(jax.random.fold_in(key_of[4], 71), 0),
        "solid_mask": draw_solid_mask(jax.random.fold_in(key_of[4], 71), 0),
        "link_flags": draw_link_flags(jax.random.fold_in(key_of[4], 71), 0),
    }


flow_velocity = np.array([[0, 0, 0], [1, 0, 0], [-1, 0, 0], [0, 1, 0], [0, -1, 0], [0, 0, 1], [0, 0, -1], [1, 1, 0], [-1, -1, 0], [1, -1, 0], [-1, 1, 0], [1, 0, 1], [-1, 0, -1], [1, 0, -1], [-1, 0, 1], [0, 1, 1], [0, -1, -1], [0, 1, -1], [0, -1, 1]])
flow_reverse = np.array([0, 2, 1, 4, 3, 6, 5, 8, 7, 10, 9, 12, 11, 14, 13, 16, 15, 18, 17])
flow_weight = np.array([1.0 / 3.0] + [1.0 / 18.0] * 6 + [1.0 / 36.0] * 12)
heat_velocity = np.array([[0, 0, 0], [1, 0, 0], [-1, 0, 0], [0, 1, 0], [0, -1, 0], [0, 0, 1], [0, 0, -1]])
heat_reverse = np.array([0, 2, 1, 4, 3, 6, 5])
thermal_quadrature_share = np.array([0.25] + [0.125] * 6)
omega_plus = 1.25
omega_minus = 1.0 / 1.125
body_force = 0.001


def vertical_slot(values):
    return jnp.asarray(np.asarray(values), jnp.float32).reshape(-1, 1, 1, 1)


def collide(flow_pops, thermal_distributions, solid_mask):
    is_fluid = solid_mask == 0
    quadrature_shares = vertical_slot(flow_weight)
    along_x = vertical_slot(flow_velocity[:, 0])
    along_y = vertical_slot(flow_velocity[:, 1])
    along_z = vertical_slot(flow_velocity[:, 2])
    density = jnp.sum(flow_pops, axis=0)
    speed_x = (jnp.sum(along_x * flow_pops, axis=0) + 0.5 * body_force) / density
    speed_y = jnp.sum(along_y * flow_pops, axis=0) / density
    speed_z = jnp.sum(along_z * flow_pops, axis=0) / density
    projected = along_x * speed_x + along_y * speed_y + along_z * speed_z
    squared = speed_x * speed_x + speed_y * speed_y + speed_z * speed_z
    balance = quadrature_shares * density * (1.0 + 3.0 * projected + 4.5 * projected * projected - 1.5 * squared)
    mirrored = flow_pops[flow_reverse]
    balance_mirror = balance[flow_reverse]
    relaxed = (flow_pops - omega_plus * 0.5 * (flow_pops + mirrored - balance - balance_mirror)
               - omega_minus * 0.5 * (flow_pops - mirrored - balance + balance_mirror)
               + 3.0 * body_force * quadrature_shares * along_x)
    relaxed = jnp.where(is_fluid, relaxed, quadrature_shares)
    node_warmth = jnp.sum(thermal_distributions, axis=0)
    moving_x = jnp.where(is_fluid, speed_x, 0.0)
    moving_y = jnp.where(is_fluid, speed_y, 0.0)
    moving_z = jnp.where(is_fluid, speed_z, 0.0)
    thermal_directed_flux = (vertical_slot(heat_velocity[:, 0]) * moving_x + vertical_slot(heat_velocity[:, 1]) * moving_y
                  + vertical_slot(heat_velocity[:, 2]) * moving_z)
    thermal_rest_state = vertical_slot(thermal_quadrature_share) * node_warmth * (1.0 + 4.0 * thermal_directed_flux)
    heat_rate = jnp.where(is_fluid, 1.2, jnp.where(solid_mask == 1, 0.7, 1.6))
    heat_relaxed = thermal_distributions - heat_rate * (thermal_distributions - thermal_rest_state)
    return jnp.concatenate([relaxed, heat_relaxed], axis=0)


def stream(padded, link_flags, x_cells, y_cells, width_x, width_y):
    rows = padded.shape[2] - 2
    cols = padded.shape[3] - 2
    centre = padded[:, :, 1:rows + 1, 1:cols + 1]

    def pulled(index, velocity):
        step_x, step_y, step_z = [int(entry) for entry in velocity]
        segment = padded[index, :, 1 - step_x:1 - step_x + rows, 1 - step_y:1 - step_y + cols]
        return jnp.roll(segment, step_z, axis=0)

    flows = [centre[0]]
    for link in range(1, 19):
        flows.append(jnp.where(link_flags[link - 1] == 1, centre[int(flow_reverse[link])], pulled(link, flow_velocity[link])))
    heats = [centre[19]]
    for link in range(1, 7):
        step_x, step_y, step_z = [int(entry) for entry in heat_velocity[link]]
        outside = ((x_cells - step_x < 0) | (x_cells - step_x >= width_x)
                   | (y_cells - step_y < 0) | (y_cells - step_y >= width_y))
        heats.append(jnp.where(outside, centre[19 + int(heat_reverse[link])], pulled(19 + link, heat_velocity[link])))
    return jnp.stack(flows), jnp.stack(heats)


def reference(flow_pops, thermal_distributions, solid_mask, link_flags):
    rows = flow_pops.shape[2]
    cols = flow_pops.shape[3]
    x_cells = jnp.arange(rows, dtype=jnp.int32).reshape(1, rows, 1)
    y_cells = jnp.arange(cols, dtype=jnp.int32).reshape(1, 1, cols)
    for step in range(STEPS):
        relaxed = collide(flow_pops, thermal_distributions, solid_mask)
        padded = jnp.pad(relaxed, ((0, 0), (0, 0), (1, 1), (1, 1)))
        flow_pops, thermal_distributions = stream(padded, link_flags, x_cells, y_cells, rows, cols)
    return flow_pops, thermal_distributions
```

```python
import functools

import jax
import jax.numpy as jnp
import numpy as np
from jax import lax
from jax.experimental import pallas as pl
from jax.experimental.pallas import tpu as pltpu
from jax.sharding import PartitionSpec as P

STEPS = 12
VEL = [
    (0, 0, 0), (1, 0, 0), (-1, 0, 0), (0, 1, 0), (0, -1, 0), (0, 0, 1), (0, 0, -1),
    (1, 1, 0), (-1, -1, 0), (1, -1, 0), (-1, 1, 0), (1, 0, 1), (-1, 0, -1),
    (1, 0, -1), (-1, 0, 1), (0, 1, 1), (0, -1, -1), (0, 1, -1), (0, -1, 1),
]
OPP = [0, 2, 1, 4, 3, 6, 5, 8, 7, 10, 9, 12, 11, 14, 13, 16, 15, 18, 17]
WEIGHT = [1.0 / 3.0] + [1.0 / 18.0] * 6 + [1.0 / 36.0] * 12
NF = 19
NP = 26
CVEL = VEL + VEL[:7]
COPP = OPP + [NF + OPP[i] for i in range(7)]
FORCE = 0.001
L = 128
S = 8
PER_TILE = 8


def outgoing(axis, sign):
    return [q for q in range(NP) if CVEL[q][axis] == sign]


COLS = {1: outgoing(1, 1), -1: outgoing(1, -1)}
ROWS = {1: outgoing(0, 1), -1: outgoing(0, -1)}
DIRS = [(1, 0), (-1, 0), (0, 1), (1, 1), (-1, 1), (0, -1), (1, -1), (-1, -1)]


def collide_tile(f, phase):
    fluid = phase == 0
    s = {}
    d = {}
    for q in range(1, NF, 2):
        s[q] = f[q] + f[q + 1]
        d[q] = f[q] - f[q + 1]
    rho = f[0] + (((s[1] + s[3]) + (s[5] + s[7])) + ((s[9] + s[11]) + (s[13] + s[15])) + s[17])
    jx = (d[1] + d[7]) + (d[9] + d[11]) + (d[13] + 0.5 * FORCE)
    jy = (d[3] + d[7]) + (d[15] - d[9]) + d[17]
    jz = (d[5] + d[11]) + (d[15] - d[13]) - d[17]
    inv = 1.0 / rho
    ux, uy, uz = jx * inv, jy * inv, jz * inv
    xx, yy, zz = jx * ux, jy * uy, jz * uz
    base = rho - 1.5 * ((xx + yy) + zz)
    wa, wd = 1.25 / 18.0, 1.25 / 36.0
    rest = base * (1.25 / 3.0) - 0.25 * f[0]
    axis_base = base * wa
    diag_base = base * wd
    ka = 4.5 * wa
    kd = 4.5 * wd
    even = {
        1: axis_base + ka * xx,
        3: axis_base + ka * yy,
        5: axis_base + ka * zz,
    }
    dxx, dyy, dzz = kd * xx, kd * yy, kd * zz
    for pair, sq, cross in (
        ((7, 9), dxx + dyy, (2.0 * kd) * jx * uy),
        ((11, 13), dxx + dzz, (2.0 * kd) * jx * uz),
        ((15, 17), dyy + dzz, (2.0 * kd) * jy * uz),
    ):
        both = diag_base + sq
        even[pair[0]] = both + cross
        even[pair[1]] = both - cross
    om = 1.0 / 1.125
    oa = 3.0 * om / 18.0
    od = 3.0 * om / 36.0
    ax, ay, az = oa * jx, oa * jy, oa * jz
    bx, by, bz = od * jx, od * jy, od * jz
    ax = ax + 3.0 * FORCE / 18.0
    bx = bx + 3.0 * FORCE / 36.0
    odd = {
        1: ax, 3: ay, 5: az,
        7: bx + by, 9: bx - by, 11: bx + bz, 13: bx - bz, 15: by + bz, 17: by - bz,
    }
    half = 0.5 - 0.5 * om
    out = [None] * NP
    out[0] = jnp.where(fluid, rest, WEIGHT[0])
    for q in range(1, NF, 2):
        even_q = even[q] - 0.125 * s[q]
        odd_q = odd[q] + half * d[q]
        out[q] = jnp.where(fluid, even_q + odd_q, WEIGHT[q])
        out[q + 1] = jnp.where(fluid, even_q - odd_q, WEIGHT[q])
    g = f[NF:]
    rate = jnp.where(fluid, 1.2, jnp.where(phase == 1, 0.7, 1.6))
    keep = 1.0 - rate
    theta = ((g[0] + g[1]) + (g[2] + g[3])) + ((g[4] + g[5]) + g[6])
    share = theta * (rate * 0.125)
    out[NF] = keep * g[0] + 2.0 * share
    moved = jnp.where(fluid, 4.0 * share, 0.0)
    for i, u in ((1, ux), (3, uy), (5, uz)):
        flux = jnp.where(fluid, moved * u, 0.0)
        out[NF + i] = keep * g[i] + (share + flux)
        out[NF + i + 1] = keep * g[i + 1] + (share - flux)
    return out


def kernel(
    gx_n, gy_n, unroll,
    flow_ref, heat_ref, phase_ref, flag_ref, flow_out, heat_out,
    fs, send_cols, send_rows, recv_cols, recv_rows, halo, send_sem, recv_sem,
):
    layers, rows = flow_ref.shape[1], flow_ref.shape[2]
    groups = rows // S
    tiles = send_cols.shape[1] // S
    per_group = len(COLS[1]) * layers
    extra = PER_TILE * per_group
    gx = lax.axis_index("gx")
    gy = lax.axis_index("gy")
    lane = lax.broadcasted_iota(jnp.int32, (S, L), 1)
    sub = lax.broadcasted_iota(jnp.int32, (S, L), 0)

    def exists(dx, dy):
        x, y = gx + dx, gy + dy
        return (x >= 0) & (x < gx_n) & (y >= 0) & (y < gy_n)

    def copy(k, slot):
        dx, dy = DIRS[k]
        if dy == 0:
            src = send_rows.at[k]
            dst = recv_rows.at[slot, k]
        else:
            src = send_cols.at[0 if dy == 1 else 1]
            dst = recv_cols.at[slot, k - 2]
        return pltpu.make_async_remote_copy(
            src_ref=src, dst_ref=dst,
            send_sem=send_sem.at[k], recv_sem=recv_sem.at[slot, k],
            device_id={"gx": gx + dx, "gy": gy + dy},
            device_id_type=pl.DeviceIdType.MESH,
        )

    def tile_rows(g):
        return pl.multiple_of(g * S, S)

    def collide_store(dst, g, z, f):
        out = collide_tile(f, phase_ref[z, pl.ds(tile_rows(g), S), :])
        for q in range(NP):
            fs[dst, q, z, pl.ds(tile_rows(g) + S, S), :] = out[q]

    def over_groups(body):
        def trip(c, carry):
            for j in range(unroll):
                body(c * unroll + j)
            return carry
        lax.fori_loop(0, groups // unroll, trip, 0)

    def pack_and_send(dst, slot):
        for k, sign in ((0, 1), (1, -1)):
            row = S + rows - 1 if sign == 1 else S
            for i, q in enumerate(ROWS[sign]):
                for z in range(layers):
                    send_rows[k, pl.ds(i * layers + z, 1), :] = fs[dst, q, z, pl.ds(row, 1), :]
        for k in (0, 1):
            @pl.when(exists(*DIRS[k]))
            def _(k=k):
                copy(k, slot).start()
        for side, sign in ((0, 1), (1, -1)):
            for t in range(tiles):
                acc = [jnp.zeros((S, L), jnp.float32) for _ in range(4)]
                n = 0

                def place(q, z, g, at):
                    nonlocal n
                    v = fs[dst, q, z, pl.ds(S + g * S - CVEL[q][0], S), :]
                    shift = (at + 1) % L if sign == 1 else at
                    if shift:
                        v = pltpu.roll(v, shift, 1)
                    acc[n % 4] = jnp.where(lane == at, v, acc[n % 4])
                    n += 1

                for i, q in enumerate(COLS[sign]):
                    for z in range(layers):
                        p = i * layers + z
                        for g in range(t * PER_TILE, min(groups, (t + 1) * PER_TILE)):
                            place(q, z, g, (g % PER_TILE) * per_group + p)
                        if t == 0 and CVEL[q][0]:
                            place(q, z, groups if CVEL[q][0] == 1 else -1, extra + p)
                send_cols[side, pl.ds(t * S, S), :] = (acc[0] + acc[1]) + (acc[2] + acc[3])
            for k, (dx, dy) in enumerate(DIRS):
                if dy == sign:
                    @pl.when(exists(dx, dy))
                    def _(k=k):
                        copy(k, slot).start()

    def receive(src, slot):
        for k, (dx, dy) in enumerate(DIRS):
            @pl.when(exists(dx, dy))
            def _(k=k):
                copy(k, slot).wait_send()

            @pl.when(exists(-dx, -dy))
            def _(k=k):
                copy(k, slot).wait_recv()
        for k, sign in ((0, 1), (1, -1)):
            row = S - 1 if sign == 1 else S + rows
            edge = S if sign == 1 else S + rows - 1

            @pl.when(exists(-sign, 0))
            def _(k=k, sign=sign, row=row):
                for i, q in enumerate(ROWS[sign]):
                    for z in range(layers):
                        fs[src, q, z, pl.ds(row, 1), :] = recv_rows[slot, k, pl.ds(i * layers + z, 1), :]

            @pl.when(jnp.logical_not(exists(-sign, 0)))
            def _(sign=sign, row=row, edge=edge):
                for q in ROWS[sign]:
                    if q >= NF:
                        for z in range(layers):
                            fs[src, q, z, pl.ds(row, 1), :] = fs[src, COPP[q], z, pl.ds(edge, 1), :]
        for side, sign in ((0, 1), (1, -1)):
            first = DIRS.index((0, sign)) - 2
            for t in range(tiles):
                v = recv_cols[slot, first, pl.ds(t * S, S), :]
                for i, q in enumerate(COLS[sign]):
                    cx = CVEL[q][0]
                    if not cx:
                        continue
                    diag = DIRS.index((cx, sign)) - 2
                    g = 0 if cx == 1 else groups - 1
                    if g // PER_TILE != t:
                        continue
                    at = (g % PER_TILE) * per_group + i * layers
                    w = recv_cols[slot, diag, pl.ds(0, S), :]
                    shift = ((g % PER_TILE) * per_group - extra) % L
                    if shift:
                        w = pltpu.roll(w, shift, 1)
                    corner = (sub == (0 if cx == 1 else S - 1)) & (lane >= at) & (lane < at + layers)
                    v = jnp.where(corner, w, v)
                halo[side, pl.ds(t * S, S), :] = v

    def stream_tile(src, g, z):
        r = tile_rows(g)
        t = tile_rows(g // PER_TILE) if tiles > 1 else 0
        first = (g % PER_TILE) * per_group
        own = [fs[src, q, z, pl.ds(r + S, S), :] for q in range(NP)]
        packed = {1: halo[0, pl.ds(t, S), :], -1: halo[1, pl.ds(t, S), :]}
        f = []
        for q in range(NP):
            cx, cy, cz = CVEL[q]
            zs = (z - cz) % layers
            if (cx, cy, cz) == (0, 0, 0):
                f.append(own[q])
                continue
            v = fs[src, q, zs, pl.ds(r + S - cx, S), :]
            if cy:
                edge = 0 if cy == 1 else L - 1
                p = COLS[cy].index(q) * layers + zs
                w = pltpu.roll(packed[cy], (2 * L + edge - p - first) % L, 1)
                v = jnp.where(lane == edge, w, pltpu.roll(v, cy % L, 1))
            if q < NF:
                v = jnp.where(flag_ref[q - 1, z, pl.ds(r, S), :] == 1, own[COPP[q]], v)
            elif cy:
                last = (gy == 0) if cy == 1 else (gy == gy_n - 1)
                wall = (lane == edge) & jnp.broadcast_to(last, (S, L))
                v = jnp.where(wall, own[COPP[q]], v)
            f.append(v)
        return f

    for k in range(2):
        send_rows[k] = jnp.zeros(send_rows.shape[1:], jnp.float32)
    for b in range(2):
        recv_cols[b] = jnp.zeros(recv_cols.shape[1:], jnp.float32)
        recv_rows[b] = jnp.zeros(recv_rows.shape[1:], jnp.float32)
        for q in range(NP):
            for z in range(layers):
                fs[b, q, z, pl.ds(0, S), :] = jnp.zeros((S, L), jnp.float32)
                fs[b, q, z, pl.ds(S + rows, S), :] = jnp.zeros((S, L), jnp.float32)

    barrier = pltpu.get_barrier_semaphore()
    count = jnp.int32(0)
    for dx, dy in DIRS:
        there = exists(dx, dy)

        @pl.when(there)
        def _(dx=dx, dy=dy):
            pl.semaphore_signal(
                barrier, inc=1, device_id={"gx": gx + dx, "gy": gy + dy},
                device_id_type=pl.DeviceIdType.MESH,
            )
        count = count + jnp.where(there, 1, 0)

    def first_collide(g):
        r = tile_rows(g)
        for z in range(layers):
            f = [flow_ref[q, z, pl.ds(r, S), :] for q in range(NF)]
            f += [heat_ref[q, z, pl.ds(r, S), :] for q in range(NP - NF)]
            collide_store(0, g, z, f)

    over_groups(first_collide)
    pl.semaphore_wait(barrier, count)
    pack_and_send(0, 0)

    def advance(e, carry):
        src = lax.rem(e - 1, 2)
        dst = lax.rem(e, 2)
        receive(src, src)

        def group(g):
            for z in range(layers):
                collide_store(dst, g, z, stream_tile(src, g, z))

        over_groups(group)
        pack_and_send(dst, dst)
        return carry

    lax.fori_loop(1, STEPS, advance, 0)
    end = (STEPS - 1) % 2
    receive(end, end)

    def finish(g):
        r = tile_rows(g)
        for z in range(layers):
            f = stream_tile(end, g, z)
            for q in range(NF):
                flow_out[q, z, pl.ds(r, S), :] = f[q]
            for q in range(NF, NP):
                heat_out[q - NF, z, pl.ds(r, S), :] = f[q]

    over_groups(finish)


def per_device(flow_pops, thermal_distributions, solid_mask, link_flags):
    layers, rows, cols = flow_pops.shape[1:]
    assert cols == L and rows % S == 0
    gx_n, gy_n = lax.axis_size("gx"), lax.axis_size("gy")
    groups = rows // S
    tiles = -(-groups // PER_TILE)
    row_slots = -(-len(ROWS[1]) * layers // S) * S
    vmem = pl.BlockSpec(memory_space=pltpu.VMEM)
    unroll = 2 if groups % 2 == 0 else 1
    return pl.pallas_call(
        functools.partial(kernel, gx_n, gy_n, unroll),
        out_shape=(
            jax.ShapeDtypeStruct(flow_pops.shape, jnp.float32),
            jax.ShapeDtypeStruct(thermal_distributions.shape, jnp.float32),
        ),
        in_specs=[vmem] * 4,
        out_specs=(vmem, vmem),
        scratch_shapes=[
            pltpu.VMEM((2, NP, layers, rows + 2 * S, L), jnp.float32),
            pltpu.VMEM((2, tiles * S, L), jnp.float32),
            pltpu.VMEM((2, row_slots, L), jnp.float32),
            pltpu.VMEM((2, 6, tiles * S, L), jnp.float32),
            pltpu.VMEM((2, 2, row_slots, L), jnp.float32),
            pltpu.VMEM((2, tiles * S, L), jnp.float32),
            pltpu.SemaphoreType.DMA((len(DIRS),)),
            pltpu.SemaphoreType.DMA((2, len(DIRS))),
        ],
        compiler_params=pltpu.CompilerParams(
            collective_id=0, has_side_effects=True, vmem_limit_bytes=48 * 1024 * 1024,
        ),
    )(flow_pops, thermal_distributions, solid_mask, link_flags)


def solution(mesh):
    placed = (
        P(None, None, "gx", "gy"),
        P(None, None, "gx", "gy"),
        P(None, "gx", "gy"),
        P(None, None, "gx", "gy"),
    )
    return jax.shard_map(
        per_device,
        mesh=mesh,
        in_specs=placed,
        out_specs=(P(None, None, "gx", "gy"), P(None, None, "gx", "gy")),
        check_vma=False,
    )
```

```python
import functools

import jax
import jax.numpy as jnp
from jax import lax
from jax.experimental import pallas as pl
from jax.experimental.pallas import tpu as pltpu
from jax.sharding import PartitionSpec as P

STEPS = 12
VEL = [
    (0, 0, 0), (1, 0, 0), (-1, 0, 0), (0, 1, 0), (0, -1, 0), (0, 0, 1), (0, 0, -1),
    (1, 1, 0), (-1, -1, 0), (1, -1, 0), (-1, 1, 0), (1, 0, 1), (-1, 0, -1),
    (1, 0, -1), (-1, 0, 1), (0, 1, 1), (0, -1, -1), (0, 1, -1), (0, -1, 1),
]
OPP = [0, 2, 1, 4, 3, 6, 5, 8, 7, 10, 9, 12, 11, 14, 13, 16, 15, 18, 17]
WEIGHT = [1.0 / 3.0] + [1.0 / 18.0] * 6 + [1.0 / 36.0] * 12
NF = 19
NP = 26
CVEL = VEL + VEL[:7]
COPP = OPP + [NF + OPP[i] for i in range(7)]
FORCE = 0.001
L = 128
S = 8
CHUNKS = 4


def outgoing(axis, sign):
    return [q for q in range(NP) if CVEL[q][axis] == sign]


COLS = {1: outgoing(1, 1), -1: outgoing(1, -1)}
ROWS = {1: outgoing(0, 1), -1: outgoing(0, -1)}
DIRS = [(1, 0), (-1, 0), (0, 1), (1, 1), (-1, 1), (0, -1), (1, -1), (-1, -1)]


def collide_tile(f, phase):
    fluid = phase == 0
    s = {}
    d = {}
    for q in range(1, NF, 2):
        s[q] = f[q] + f[q + 1]
        d[q] = f[q] - f[q + 1]
    rho = f[0] + (((s[1] + s[3]) + (s[5] + s[7])) + ((s[9] + s[11]) + (s[13] + s[15])) + s[17])
    jx = (d[1] + d[7]) + (d[9] + d[11]) + (d[13] + 0.5 * FORCE)
    jy = (d[3] + d[7]) + (d[15] - d[9]) + d[17]
    jz = (d[5] + d[11]) + (d[15] - d[13]) - d[17]
    inv = 1.0 / rho
    ux, uy, uz = jx * inv, jy * inv, jz * inv
    xx, yy, zz = jx * ux, jy * uy, jz * uz
    base = rho - 1.5 * ((xx + yy) + zz)
    wa, wd = 1.25 / 18.0, 1.25 / 36.0
    rest = base * (1.25 / 3.0) - 0.25 * f[0]
    axis_base = base * wa
    diag_base = base * wd
    ka = 4.5 * wa
    kd = 4.5 * wd
    even = {
        1: axis_base + ka * xx,
        3: axis_base + ka * yy,
        5: axis_base + ka * zz,
    }
    dxx, dyy, dzz = kd * xx, kd * yy, kd * zz
    for pair, sq, cross in (
        ((7, 9), dxx + dyy, (2.0 * kd) * jx * uy),
        ((11, 13), dxx + dzz, (2.0 * kd) * jx * uz),
        ((15, 17), dyy + dzz, (2.0 * kd) * jy * uz),
    ):
        both = diag_base + sq
        even[pair[0]] = both + cross
        even[pair[1]] = both - cross
    om = 1.0 / 1.125
    oa = 3.0 * om / 18.0
    od = 3.0 * om / 36.0
    ax, ay, az = oa * jx, oa * jy, oa * jz
    bx, by, bz = od * jx, od * jy, od * jz
    ax = ax + 3.0 * FORCE / 18.0
    bx = bx + 3.0 * FORCE / 36.0
    odd = {
        1: ax, 3: ay, 5: az,
        7: bx + by, 9: bx - by, 11: bx + bz, 13: bx - bz, 15: by + bz, 17: by - bz,
    }
    half = 0.5 - 0.5 * om
    out = [None] * NP
    out[0] = jnp.where(fluid, rest, WEIGHT[0])
    for q in range(1, NF, 2):
        even_q = even[q] - 0.125 * s[q]
        odd_q = odd[q] + half * d[q]
        out[q] = jnp.where(fluid, even_q + odd_q, WEIGHT[q])
        out[q + 1] = jnp.where(fluid, even_q - odd_q, WEIGHT[q])
    g = f[NF:]
    rate = jnp.where(fluid, 1.2, jnp.where(phase == 1, 0.7, 1.6))
    keep = 1.0 - rate
    theta = ((g[0] + g[1]) + (g[2] + g[3])) + ((g[4] + g[5]) + g[6])
    share = theta * (rate * 0.125)
    out[NF] = keep * g[0] + 2.0 * share
    moved = jnp.where(fluid, 4.0 * share, 0.0)
    for i, u in ((1, ux), (3, uy), (5, uz)):
        flux = jnp.where(fluid, moved * u, 0.0)
        out[NF + i] = keep * g[i] + (share + flux)
        out[NF + i + 1] = keep * g[i + 1] + (share - flux)
    return out


def chunks_of(groups):
    m = groups // (2 * CHUNKS)
    return [
        [g for a in range(c * m, (c + 1) * m) for g in (groups // 2 - 1 - a, groups // 2 + a)]
        for c in range(CHUNKS)
    ]


def kernel(
    gx_n, gy_n,
    flow_in, heat_in, phase_in, flag_in, flow_out, heat_out,
    flow_ref, heat_ref, phase_ref, flag_ref,
    fs, send_cols, send_rows, recv_cols, recv_rows, recv_diag,
    send_sem, recv_sem, in_sem, out_sem,
):
    layers, rows = flow_ref.shape[1], flow_ref.shape[2]
    groups = rows // S
    chunks = chunks_of(groups)
    per_group = len(COLS[1]) * layers
    extra = len(chunks[0]) * per_group
    gx = lax.axis_index("gx")
    gy = lax.axis_index("gy")
    lane = lax.broadcasted_iota(jnp.int32, (S, L), 1)
    sub = lax.broadcasted_iota(jnp.int32, (S, L), 0)

    loads = []
    for src, dst, step in ((flow_in, flow_ref, 5), (heat_in, heat_ref, 4), (phase_in, phase_ref, 2), (flag_in, flag_ref, 3)):
        pieces = []
        for at in range(0, dst.shape[0], step):
            part = pl.ds(at, min(step, dst.shape[0] - at))
            n = sum(len(p) for p in loads) + len(pieces)
            pieces.append(pltpu.make_async_copy(src.at[part], dst.at[part], in_sem.at[n]))
        loads.append(pieces)
    for pieces in loads:
        for piece in pieces:
            piece.start()

    def exists(dx, dy):
        x, y = gx + dx, gy + dy
        return (x >= 0) & (x < gx_n) & (y >= 0) & (y < gy_n)

    ids = {}
    for sign in (1, -1):
        ids["row", sign] = len(ids)
    for sign in (1, -1):
        for c in range(CHUNKS):
            ids["col", sign, c] = len(ids)
    for dx in (1, -1):
        for dy in (1, -1):
            ids["diag", dx, dy] = len(ids)

    def direction(m):
        if m[0] == "row":
            return m[1], 0
        if m[0] == "col":
            return 0, m[1]
        return m[1], m[2]

    def side(sign):
        return 0 if sign == 1 else 1

    def diag_slot(dx, dy):
        return side(dx) * 2 + side(dy)

    def copy(m, slot):
        dx, dy = direction(m)
        if m[0] == "row":
            src, dst = send_rows.at[side(dx)], recv_rows.at[slot, side(dx)]
        elif m[0] == "col":
            src, dst = send_cols.at[side(dy), m[2]], recv_cols.at[slot, side(dy), m[2]]
        else:
            src, dst = send_cols.at[side(dy), CHUNKS - 1], recv_diag.at[slot, diag_slot(dx, dy)]
        return pltpu.make_async_remote_copy(
            src_ref=src, dst_ref=dst,
            send_sem=send_sem.at[ids[m]], recv_sem=recv_sem.at[slot, ids[m]],
            device_id={"gx": gx + dx, "gy": gy + dy},
            device_id_type=pl.DeviceIdType.MESH,
        )

    def start(m, slot):
        @pl.when(exists(*direction(m)))
        def _():
            copy(m, slot).start()

    def finish_message(m, slot):
        dx, dy = direction(m)

        @pl.when(exists(dx, dy))
        def _():
            copy(m, slot).wait_send()

        @pl.when(exists(-dx, -dy))
        def _():
            copy(m, slot).wait_recv()

    def send_outer_rows(dst, slot):
        for sign in (1, -1):
            row = S + rows - 1 if sign == 1 else S
            for i, q in enumerate(ROWS[sign]):
                for z in range(layers):
                    send_rows[side(sign), pl.ds(i * layers + z, 1), :] = fs[dst, q, z, pl.ds(row, 1), :]
        for sign in (1, -1):
            start(("row", sign), slot)

    def send_columns(dst, slot, c):
        for sign in (1, -1):
            acc = [jnp.zeros((S, L), jnp.float32) for _ in range(4)]
            n = 0

            def place(q, z, g, at):
                nonlocal n
                v = fs[dst, q, z, pl.ds(S + g * S - CVEL[q][0], S), :]
                shift = (at + 1) % L if sign == 1 else at
                if shift:
                    v = pltpu.roll(v, shift, 1)
                acc[n % 4] = jnp.where(lane == at, v, acc[n % 4])
                n += 1

            for i, q in enumerate(COLS[sign]):
                for z in range(layers):
                    p = i * layers + z
                    for k, g in enumerate(chunks[c]):
                        place(q, z, g, k * per_group + p)
                    if c == CHUNKS - 1 and CVEL[q][0]:
                        place(q, z, groups if CVEL[q][0] == 1 else -1, extra + p)
            send_cols[side(sign), c] = (acc[0] + acc[1]) + (acc[2] + acc[3])
        for sign in (1, -1):
            start(("col", sign, c), slot)
        if c == CHUNKS - 1:
            for dx in (1, -1):
                for dy in (1, -1):
                    start(("diag", dx, dy), slot)

    def receive_outer_rows(src, slot):
        for sign in (1, -1):
            finish_message(("row", sign), slot)
            row = S - 1 if sign == 1 else S + rows
            edge = S if sign == 1 else S + rows - 1

            @pl.when(exists(-sign, 0))
            def _(sign=sign, row=row):
                for i, q in enumerate(ROWS[sign]):
                    for z in range(layers):
                        fs[src, q, z, pl.ds(row, 1), :] = recv_rows[slot, side(sign), pl.ds(i * layers + z, 1), :]

            @pl.when(jnp.logical_not(exists(-sign, 0)))
            def _(sign=sign, row=row, edge=edge):
                for q in ROWS[sign]:
                    if q >= NF:
                        for z in range(layers):
                            fs[src, q, z, pl.ds(row, 1), :] = fs[src, COPP[q], z, pl.ds(edge, 1), :]

    def receive(src, slot, c):
        for sign in (1, -1):
            finish_message(("col", sign, c), slot)
        if c == CHUNKS - 1:
            receive_outer_rows(src, slot)
            for dx in (1, -1):
                for dy in (1, -1):
                    finish_message(("diag", dx, dy), slot)
        packed = {}
        for sign in (1, -1):
            v = recv_cols[slot, side(sign), c]
            if c == CHUNKS - 1:
                for i, q in enumerate(COLS[sign]):
                    cx = CVEL[q][0]
                    if not cx:
                        continue
                    first = chunks[c].index(0 if cx == 1 else groups - 1) * per_group
                    at = first + i * layers
                    w = pltpu.roll(recv_diag[slot, diag_slot(cx, sign)], (first - extra) % L, 1)
                    corner = (sub == (0 if cx == 1 else S - 1)) & (lane >= at) & (lane < at + layers)
                    v = jnp.where(corner, w, v)
            packed[sign] = v
        return packed

    def stream_tile(src, g, z, packed, first):
        r = g * S
        own = [fs[src, q, z, pl.ds(r + S, S), :] for q in range(NP)]
        f = []
        for q in range(NP):
            cx, cy, cz = CVEL[q]
            zs = (z - cz) % layers
            if (cx, cy, cz) == (0, 0, 0):
                f.append(own[q])
                continue
            v = fs[src, q, zs, pl.ds(r + S - cx, S), :]
            if cy:
                edge = 0 if cy == 1 else L - 1
                p = COLS[cy].index(q) * layers + zs
                w = packed[cy]
                shift = (edge - p - first) % L
                if shift:
                    w = pltpu.roll(w, shift, 1)
                v = jnp.where(lane == edge, w, pltpu.roll(v, cy % L, 1))
            if q < NF:
                v = jnp.where(flag_ref[q - 1, z, pl.ds(r, S), :] == 1, own[COPP[q]], v)
            elif cy:
                last = (gy == 0) if cy == 1 else (gy == gy_n - 1)
                wall = (lane == edge) & jnp.broadcast_to(last, (S, L))
                v = jnp.where(wall, own[COPP[q]], v)
            f.append(v)
        return f

    def collide_store(dst, g, z, f):
        out = collide_tile(f, phase_ref[z, pl.ds(g * S, S), :])
        for q in range(NP):
            fs[dst, q, z, pl.ds(g * S + S, S), :] = out[q]

    for k in range(2):
        send_rows[k] = jnp.zeros(send_rows.shape[1:], jnp.float32)
    for b in range(2):
        recv_rows[b] = jnp.zeros(recv_rows.shape[1:], jnp.float32)
        recv_diag[b] = jnp.zeros(recv_diag.shape[1:], jnp.float32)
        recv_cols[b] = jnp.zeros(recv_cols.shape[1:], jnp.float32)
        for q in range(NP):
            for z in range(layers):
                fs[b, q, z, pl.ds(0, S), :] = jnp.zeros((S, L), jnp.float32)
                fs[b, q, z, pl.ds(S + rows, S), :] = jnp.zeros((S, L), jnp.float32)

    barrier = pltpu.get_barrier_semaphore()
    count = jnp.int32(0)
    for dx, dy in DIRS:
        there = exists(dx, dy)

        @pl.when(there)
        def _(dx=dx, dy=dy):
            pl.semaphore_signal(
                barrier, inc=1, device_id={"gx": gx + dx, "gy": gy + dy},
                device_id_type=pl.DeviceIdType.MESH,
            )
        count = count + jnp.where(there, 1, 0)
    pl.semaphore_wait(barrier, count)

    def sends_after(c, dst):
        if c == CHUNKS - 1:
            send_outer_rows(dst, dst)
        if c > 0:
            send_columns(dst, dst, c - 1)
        if c == CHUNKS - 1:
            send_columns(dst, dst, c)

    for pieces in loads[:3]:
        for piece in pieces:
            piece.wait()
    for c, members in enumerate(chunks):
        for g in members:
            for z in range(layers):
                f = [flow_ref[q, z, pl.ds(g * S, S), :] for q in range(NF)]
                f += [heat_ref[q, z, pl.ds(g * S, S), :] for q in range(NP - NF)]
                collide_store(0, g, z, f)
        sends_after(c, 0)
    for piece in loads[3]:
        piece.wait()

    def advance(e, carry):
        src = lax.rem(e - 1, 2)
        dst = lax.rem(e, 2)
        for c, members in enumerate(chunks):
            packed = receive(src, src, c)
            for k, g in enumerate(members):
                for z in range(layers):
                    collide_store(dst, g, z, stream_tile(src, g, z, packed, k * per_group))
            sends_after(c, dst)
        return carry

    lax.fori_loop(1, STEPS, advance, 0)
    end = (STEPS - 1) % 2
    stores = []
    for c, members in enumerate(chunks):
        packed = receive(end, end, c)
        for k, g in enumerate(members):
            part = pl.ds(g * S, S)
            for z in range(layers):
                f = stream_tile(end, g, z, packed, k * per_group)
                for q in range(NF):
                    flow_ref[q, z, part, :] = f[q]
                for q in range(NF, NP):
                    heat_ref[q - NF, z, part, :] = f[q]
            for i, (ref, out) in enumerate(((flow_ref, flow_out), (heat_ref, heat_out))):
                stores.append(pltpu.make_async_copy(ref.at[:, :, part], out.at[:, :, part], out_sem.at[g, i]))
                stores[-1].start()
    for store in stores:
        store.wait()


def per_device(flow_pops, thermal_distributions, solid_mask, link_flags):
    layers, rows, cols = flow_pops.shape[1:]
    groups = rows // S
    assert cols == L and rows % (2 * CHUNKS * S) == 0
    gx_n, gy_n = lax.axis_size("gx"), lax.axis_size("gy")
    row_slots = -(-len(ROWS[1]) * layers // S) * S
    messages = 2 + 2 * CHUNKS + 4
    anywhere = pl.BlockSpec(memory_space=pl.ANY)
    return pl.pallas_call(
        functools.partial(kernel, gx_n, gy_n),
        out_shape=(
            jax.ShapeDtypeStruct(flow_pops.shape, jnp.float32),
            jax.ShapeDtypeStruct(thermal_distributions.shape, jnp.float32),
        ),
        in_specs=[anywhere] * 4,
        out_specs=(anywhere, anywhere),
        scratch_shapes=[
            pltpu.VMEM(flow_pops.shape, jnp.float32),
            pltpu.VMEM(thermal_distributions.shape, jnp.float32),
            pltpu.VMEM(solid_mask.shape, jnp.int32),
            pltpu.VMEM(link_flags.shape, jnp.int32),
            pltpu.VMEM((2, NP, layers, rows + 2 * S, L), jnp.float32),
            pltpu.VMEM((2, CHUNKS, S, L), jnp.float32),
            pltpu.VMEM((2, row_slots, L), jnp.float32),
            pltpu.VMEM((2, 2, CHUNKS, S, L), jnp.float32),
            pltpu.VMEM((2, 2, row_slots, L), jnp.float32),
            pltpu.VMEM((2, 4, S, L), jnp.float32),
            pltpu.SemaphoreType.DMA((messages,)),
            pltpu.SemaphoreType.DMA((2, messages)),
            pltpu.SemaphoreType.DMA((16,)),
            pltpu.SemaphoreType.DMA((groups, 2)),
        ],
        compiler_params=pltpu.CompilerParams(
            collective_id=0, has_side_effects=True, vmem_limit_bytes=56 * 1024 * 1024,
        ),
    )(flow_pops, thermal_distributions, solid_mask, link_flags)


def solution(mesh):
    placed = (
        P(None, None, "gx", "gy"),
        P(None, None, "gx", "gy"),
        P(None, "gx", "gy"),
        P(None, None, "gx", "gy"),
    )
    return jax.shard_map(
        per_device,
        mesh=mesh,
        in_specs=placed,
        out_specs=(P(None, None, "gx", "gy"), P(None, None, "gx", "gy")),
        check_vma=False,
    )
```

```python
import functools

import jax
import jax.numpy as jnp
from jax import lax
from jax.experimental import pallas as pl
from jax.experimental.pallas import tpu as pltpu
from jax.sharding import PartitionSpec as P

STEPS = 12
VEL = [
    (0, 0, 0), (1, 0, 0), (-1, 0, 0), (0, 1, 0), (0, -1, 0), (0, 0, 1), (0, 0, -1),
    (1, 1, 0), (-1, -1, 0), (1, -1, 0), (-1, 1, 0), (1, 0, 1), (-1, 0, -1),
    (1, 0, -1), (-1, 0, 1), (0, 1, 1), (0, -1, -1), (0, 1, -1), (0, -1, 1),
]
OPP = [0, 2, 1, 4, 3, 6, 5, 8, 7, 10, 9, 12, 11, 14, 13, 16, 15, 18, 17]
WEIGHT = [1.0 / 3.0] + [1.0 / 18.0] * 6 + [1.0 / 36.0] * 12
NF = 19
NP = 26
CVEL = VEL + VEL[:7]
COPP = OPP + [NF + OPP[i] for i in range(7)]
FORCE = 0.001
L = 128
S = 8
CHUNKS = 4


def outgoing(axis, sign):
    return [q for q in range(NP) if CVEL[q][axis] == sign]


COLS = {1: outgoing(1, 1), -1: outgoing(1, -1)}
ROWS = {1: outgoing(0, 1), -1: outgoing(0, -1)}
DIRS = [(1, 0), (-1, 0), (0, 1), (1, 1), (-1, 1), (0, -1), (1, -1), (-1, -1)]


def collide_tile(f, phase):
    fluid = phase == 0
    s = {}
    d = {}
    for q in range(1, NF, 2):
        s[q] = f[q] + f[q + 1]
        d[q] = f[q] - f[q + 1]
    rho = f[0] + (((s[1] + s[3]) + (s[5] + s[7])) + ((s[9] + s[11]) + (s[13] + s[15])) + s[17])
    jx = (d[1] + d[7]) + (d[9] + d[11]) + (d[13] + 0.5 * FORCE)
    jy = (d[3] + d[7]) + (d[15] - d[9]) + d[17]
    jz = (d[5] + d[11]) + (d[15] - d[13]) - d[17]
    inv = 1.0 / rho
    ux, uy, uz = jx * inv, jy * inv, jz * inv
    xx, yy, zz = jx * ux, jy * uy, jz * uz
    base = rho - 1.5 * ((xx + yy) + zz)
    wa, wd = 1.25 / 18.0, 1.25 / 36.0
    rest = base * (1.25 / 3.0) - 0.25 * f[0]
    axis_base = base * wa
    diag_base = base * wd
    ka = 4.5 * wa
    kd = 4.5 * wd
    even = {
        1: axis_base + ka * xx,
        3: axis_base + ka * yy,
        5: axis_base + ka * zz,
    }
    dxx, dyy, dzz = kd * xx, kd * yy, kd * zz
    for pair, sq, cross in (
        ((7, 9), dxx + dyy, (2.0 * kd) * jx * uy),
        ((11, 13), dxx + dzz, (2.0 * kd) * jx * uz),
        ((15, 17), dyy + dzz, (2.0 * kd) * jy * uz),
    ):
        both = diag_base + sq
        even[pair[0]] = both + cross
        even[pair[1]] = both - cross
    om = 1.0 / 1.125
    oa = 3.0 * om / 18.0
    od = 3.0 * om / 36.0
    ax, ay, az = oa * jx, oa * jy, oa * jz
    bx, by, bz = od * jx, od * jy, od * jz
    ax = ax + 3.0 * FORCE / 18.0
    bx = bx + 3.0 * FORCE / 36.0
    odd = {
        1: ax, 3: ay, 5: az,
        7: bx + by, 9: bx - by, 11: bx + bz, 13: bx - bz, 15: by + bz, 17: by - bz,
    }
    half = 0.5 - 0.5 * om
    out = [None] * NP
    out[0] = jnp.where(fluid, rest, WEIGHT[0])
    for q in range(1, NF, 2):
        even_q = even[q] - 0.125 * s[q]
        odd_q = odd[q] + half * d[q]
        out[q] = jnp.where(fluid, even_q + odd_q, WEIGHT[q])
        out[q + 1] = jnp.where(fluid, even_q - odd_q, WEIGHT[q])
    g = f[NF:]
    rate = jnp.where(fluid, 1.2, jnp.where(phase == 1, 0.7, 1.6))
    keep = 1.0 - rate
    theta = ((g[0] + g[1]) + (g[2] + g[3])) + ((g[4] + g[5]) + g[6])
    share = theta * (rate * 0.125)
    out[NF] = keep * g[0] + 2.0 * share
    moved = jnp.where(fluid, 4.0 * share, 0.0)
    for i, u in ((1, ux), (3, uy), (5, uz)):
        flux = jnp.where(fluid, moved * u, 0.0)
        out[NF + i] = keep * g[i] + (share + flux)
        out[NF + i + 1] = keep * g[i + 1] + (share - flux)
    return out


def chunks_of(groups):
    m = groups // (2 * CHUNKS)
    return [
        [g for a in range(c * m, (c + 1) * m) for g in (groups // 2 - 1 - a, groups // 2 + a)]
        for c in range(CHUNKS)
    ]


def kernel(
    gx_n, gy_n,
    flow_in, heat_in, phase_in, flag_in, flow_out, heat_out,
    flow_ref, heat_ref, phase_ref, flag_ref,
    fs, send_cols, send_rows, recv_cols, recv_rows, recv_diag,
    send_sem, recv_sem, in_sem, mask_sem, out_sem,
):
    layers, rows = flow_ref.shape[1], flow_ref.shape[2]
    groups = rows // S
    chunks = chunks_of(groups)
    per_group = len(COLS[1]) * layers
    extra = len(chunks[0]) * per_group
    holder = {g: c for c, members in enumerate(chunks) for g in members}
    top, bottom = holder[0], holder[groups - 1]
    ready = [
        max(holder[h] for g in members for h in (g - 1, g, g + 1) if 0 <= h < groups)
        for members in chunks
    ]
    gx = lax.axis_index("gx")
    gy = lax.axis_index("gy")
    lane = lax.broadcasted_iota(jnp.int32, (S, L), 1)
    sub = lax.broadcasted_iota(jnp.int32, (S, L), 0)

    loads = {}
    for members in chunks:
        for g in members:
            part = pl.ds(g * S, S)
            loads[g] = [
                pltpu.make_async_copy(flow_in.at[:, :, part], flow_ref.at[:, :, part], in_sem.at[g, 0]),
                pltpu.make_async_copy(heat_in.at[:, :, part], heat_ref.at[:, :, part], in_sem.at[g, 1]),
            ]
    phase_load = pltpu.make_async_copy(phase_in, phase_ref, mask_sem.at[0])
    flag_loads = []
    for n, at in enumerate(range(0, flag_ref.shape[0], 6)):
        part = pl.ds(at, min(6, flag_ref.shape[0] - at))
        flag_loads.append(pltpu.make_async_copy(flag_in.at[part], flag_ref.at[part], mask_sem.at[n + 1]))
    phase_load.start()
    for members in chunks:
        for g in members:
            for piece in loads[g]:
                piece.start()
    for piece in flag_loads:
        piece.start()

    def exists(dx, dy):
        x, y = gx + dx, gy + dy
        return (x >= 0) & (x < gx_n) & (y >= 0) & (y < gy_n)

    ids = {}
    for sign in (1, -1):
        ids["row", sign] = len(ids)
    for sign in (1, -1):
        for c in range(CHUNKS):
            ids["col", sign, c] = len(ids)
    for dx in (1, -1):
        for dy in (1, -1):
            ids["diag", dx, dy] = len(ids)

    def direction(m):
        if m[0] == "row":
            return m[1], 0
        if m[0] == "col":
            return 0, m[1]
        return m[1], m[2]

    def side(sign):
        return 0 if sign == 1 else 1

    def diag_slot(dx, dy):
        return side(dx) * 2 + side(dy)

    def copy(m, slot):
        dx, dy = direction(m)
        if m[0] == "row":
            src, dst = send_rows.at[side(dx)], recv_rows.at[slot, side(dx)]
        elif m[0] == "col":
            src, dst = send_cols.at[side(dy), m[2]], recv_cols.at[slot, side(dy), m[2]]
        else:
            src, dst = send_cols.at[side(dy), bottom if dx == 1 else top], recv_diag.at[slot, diag_slot(dx, dy)]
        return pltpu.make_async_remote_copy(
            src_ref=src, dst_ref=dst,
            send_sem=send_sem.at[ids[m]], recv_sem=recv_sem.at[slot, ids[m]],
            device_id={"gx": gx + dx, "gy": gy + dy},
            device_id_type=pl.DeviceIdType.MESH,
        )

    def start(m, slot):
        @pl.when(exists(*direction(m)))
        def _():
            copy(m, slot).start()

    def wait_sent(m, slot):
        @pl.when(exists(*direction(m)))
        def _():
            copy(m, slot).wait_send()

    def wait_arrived(m, slot):
        dx, dy = direction(m)

        @pl.when(exists(-dx, -dy))
        def _():
            copy(m, slot).wait_recv()

    def send_outer_row(dst, slot, sign):
        row = S + rows - 1 if sign == 1 else S
        for i, q in enumerate(ROWS[sign]):
            for z in range(layers):
                send_rows[side(sign), pl.ds(i * layers + z, 1), :] = fs[dst, q, z, pl.ds(row, 1), :]
        start(("row", sign), slot)

    def send_columns(dst, slot, c):
        for sign in (1, -1):
            acc = [jnp.zeros((S, L), jnp.float32) for _ in range(4)]
            n = 0

            def place(q, z, g, at):
                nonlocal n
                v = fs[dst, q, z, pl.ds(S + g * S - CVEL[q][0], S), :]
                shift = (at + 1) % L if sign == 1 else at
                if shift:
                    v = pltpu.roll(v, shift, 1)
                acc[n % 4] = jnp.where(lane == at, v, acc[n % 4])
                n += 1

            for i, q in enumerate(COLS[sign]):
                for z in range(layers):
                    p = i * layers + z
                    for k, g in enumerate(chunks[c]):
                        place(q, z, g, k * per_group + p)
                    if c == bottom and CVEL[q][0] == 1:
                        place(q, z, groups, extra + p)
                    if c == top and CVEL[q][0] == -1:
                        place(q, z, -1, extra + p)
            send_cols[side(sign), c] = (acc[0] + acc[1]) + (acc[2] + acc[3])
        for sign in (1, -1):
            start(("col", sign, c), slot)
        for dx, c_out in ((1, bottom), (-1, top)):
            if c == c_out:
                for dy in (1, -1):
                    start(("diag", dx, dy), slot)

    def receive_outer_row(src, slot, sign):
        wait_arrived(("row", sign), slot)
        row = S - 1 if sign == 1 else S + rows
        edge = S if sign == 1 else S + rows - 1

        @pl.when(exists(-sign, 0))
        def _():
            for i, q in enumerate(ROWS[sign]):
                for z in range(layers):
                    fs[src, q, z, pl.ds(row, 1), :] = recv_rows[slot, side(sign), pl.ds(i * layers + z, 1), :]

        @pl.when(jnp.logical_not(exists(-sign, 0)))
        def _():
            for q in ROWS[sign]:
                if q >= NF:
                    for z in range(layers):
                        fs[src, q, z, pl.ds(row, 1), :] = fs[src, COPP[q], z, pl.ds(edge, 1), :]

    def receive(src, slot, c):
        for sign in (1, -1):
            wait_sent(("col", sign, c), slot)
            wait_arrived(("col", sign, c), slot)
        for dx, c_out, c_in in ((1, bottom, top), (-1, top, bottom)):
            if c == c_out:
                wait_sent(("row", dx), slot)
                for dy in (1, -1):
                    wait_sent(("diag", dx, dy), slot)
            if c == c_in:
                receive_outer_row(src, slot, dx)
                for dy in (1, -1):
                    wait_arrived(("diag", dx, dy), slot)
        packed = {}
        for sign in (1, -1):
            v = recv_cols[slot, side(sign), c]
            if c in (top, bottom):
                for i, q in enumerate(COLS[sign]):
                    cx = CVEL[q][0]
                    if not cx or c != (top if cx == 1 else bottom):
                        continue
                    first = chunks[c].index(0 if cx == 1 else groups - 1) * per_group
                    at = first + i * layers
                    w = pltpu.roll(recv_diag[slot, diag_slot(cx, sign)], (first - extra) % L, 1)
                    corner = (sub == (0 if cx == 1 else S - 1)) & (lane >= at) & (lane < at + layers)
                    v = jnp.where(corner, w, v)
            packed[sign] = v
        return packed

    def stream_tile(src, g, z, packed, first):
        r = g * S
        own = [fs[src, q, z, pl.ds(r + S, S), :] for q in range(NP)]
        f = []
        for q in range(NP):
            cx, cy, cz = CVEL[q]
            zs = (z - cz) % layers
            if (cx, cy, cz) == (0, 0, 0):
                f.append(own[q])
                continue
            v = fs[src, q, zs, pl.ds(r + S - cx, S), :]
            if cy:
                edge = 0 if cy == 1 else L - 1
                p = COLS[cy].index(q) * layers + zs
                w = packed[cy]
                shift = (edge - p - first) % L
                if shift:
                    w = pltpu.roll(w, shift, 1)
                v = jnp.where(lane == edge, w, pltpu.roll(v, cy % L, 1))
            if q < NF:
                v = jnp.where(flag_ref[q - 1, z, pl.ds(r, S), :] == 1, own[COPP[q]], v)
            elif cy:
                last = (gy == 0) if cy == 1 else (gy == gy_n - 1)
                wall = (lane == edge) & jnp.broadcast_to(last, (S, L))
                v = jnp.where(wall, own[COPP[q]], v)
            f.append(v)
        return f

    def collide_store(dst, g, z, f):
        out = collide_tile(f, phase_ref[z, pl.ds(g * S, S), :])
        for q in range(NP):
            fs[dst, q, z, pl.ds(g * S + S, S), :] = out[q]

    for k in range(2):
        send_rows[k] = jnp.zeros(send_rows.shape[1:], jnp.float32)
    for b in range(2):
        recv_rows[b] = jnp.zeros(recv_rows.shape[1:], jnp.float32)
        recv_diag[b] = jnp.zeros(recv_diag.shape[1:], jnp.float32)
        recv_cols[b] = jnp.zeros(recv_cols.shape[1:], jnp.float32)

    barrier = pltpu.get_barrier_semaphore()
    count = jnp.int32(0)
    for dx, dy in DIRS:
        there = exists(dx, dy)

        @pl.when(there)
        def _(dx=dx, dy=dy):
            pl.semaphore_signal(
                barrier, inc=1, device_id={"gx": gx + dx, "gy": gy + dy},
                device_id_type=pl.DeviceIdType.MESH,
            )
        count = count + jnp.where(there, 1, 0)
    for b in range(2):
        for q in range(NP):
            for z in range(layers):
                fs[b, q, z, pl.ds(0, S), :] = jnp.zeros((S, L), jnp.float32)
                fs[b, q, z, pl.ds(S + rows, S), :] = jnp.zeros((S, L), jnp.float32)

    def sends_after(c, dst):
        for sign, c_out in ((1, bottom), (-1, top)):
            if c == c_out:
                send_outer_row(dst, dst, sign)
        for c_out in range(CHUNKS):
            if ready[c_out] == c:
                send_columns(dst, dst, c_out)

    phase_load.wait()
    for c, members in enumerate(chunks):
        for g in members:
            for piece in loads[g]:
                piece.wait()
        for g in members:
            for z in range(layers):
                f = [flow_ref[q, z, pl.ds(g * S, S), :] for q in range(NF)]
                f += [heat_ref[q, z, pl.ds(g * S, S), :] for q in range(NP - NF)]
                collide_store(0, g, z, f)
        if c == min(ready):
            pl.semaphore_wait(barrier, count)
        sends_after(c, 0)
    for piece in flag_loads:
        piece.wait()

    def advance(e, carry):
        src = lax.rem(e - 1, 2)
        dst = lax.rem(e, 2)
        for c, members in enumerate(chunks):
            packed = receive(src, src, c)
            for k, g in enumerate(members):
                for z in range(layers):
                    collide_store(dst, g, z, stream_tile(src, g, z, packed, k * per_group))
            sends_after(c, dst)
        return carry

    lax.fori_loop(1, STEPS, advance, 0)
    end = (STEPS - 1) % 2
    stores = []
    for c, members in enumerate(chunks):
        packed = receive(end, end, c)
        for k, g in enumerate(members):
            part = pl.ds(g * S, S)
            for z in range(layers):
                f = stream_tile(end, g, z, packed, k * per_group)
                for q in range(NF):
                    flow_ref[q, z, part, :] = f[q]
                for q in range(NF, NP):
                    heat_ref[q - NF, z, part, :] = f[q]
            for i, (ref, out) in enumerate(((flow_ref, flow_out), (heat_ref, heat_out))):
                stores.append(pltpu.make_async_copy(ref.at[:, :, part], out.at[:, :, part], out_sem.at[g, i]))
                stores[-1].start()
    for store in stores:
        store.wait()


def per_device(flow_pops, thermal_distributions, solid_mask, link_flags):
    layers, rows, cols = flow_pops.shape[1:]
    groups = rows // S
    assert cols == L and rows % (CHUNKS * S) == 0
    gx_n, gy_n = lax.axis_size("gx"), lax.axis_size("gy")
    row_slots = -(-len(ROWS[1]) * layers // S) * S
    messages = 2 + 2 * CHUNKS + 4
    anywhere = pl.BlockSpec(memory_space=pl.ANY)
    return pl.pallas_call(
        functools.partial(kernel, gx_n, gy_n),
        out_shape=(
            jax.ShapeDtypeStruct(flow_pops.shape, jnp.float32),
            jax.ShapeDtypeStruct(thermal_distributions.shape, jnp.float32),
        ),
        in_specs=[anywhere] * 4,
        out_specs=(anywhere, anywhere),
        scratch_shapes=[
            pltpu.VMEM(flow_pops.shape, jnp.float32),
            pltpu.VMEM(thermal_distributions.shape, jnp.float32),
            pltpu.VMEM(solid_mask.shape, jnp.int32),
            pltpu.VMEM(link_flags.shape, jnp.int32),
            pltpu.VMEM((2, NP, layers, rows + 2 * S, L), jnp.float32),
            pltpu.VMEM((2, CHUNKS, S, L), jnp.float32),
            pltpu.VMEM((2, row_slots, L), jnp.float32),
            pltpu.VMEM((2, 2, CHUNKS, S, L), jnp.float32),
            pltpu.VMEM((2, 2, row_slots, L), jnp.float32),
            pltpu.VMEM((2, 4, S, L), jnp.float32),
            pltpu.SemaphoreType.DMA((messages,)),
            pltpu.SemaphoreType.DMA((2, messages)),
            pltpu.SemaphoreType.DMA((groups, 2)),
            pltpu.SemaphoreType.DMA((4,)),
            pltpu.SemaphoreType.DMA((groups, 2)),
        ],
        compiler_params=pltpu.CompilerParams(
            collective_id=0, has_side_effects=True, vmem_limit_bytes=56 * 1024 * 1024,
        ),
    )(flow_pops, thermal_distributions, solid_mask, link_flags)


def solution(mesh):
    placed = (
        P(None, None, "gx", "gy"),
        P(None, None, "gx", "gy"),
        P(None, "gx", "gy"),
        P(None, None, "gx", "gy"),
    )
    return jax.shard_map(
        per_device,
        mesh=mesh,
        in_specs=placed,
        out_specs=(P(None, None, "gx", "gy"), P(None, None, "gx", "gy")),
        check_vma=False,
    )
```
